32 devices in a mesh: groups: 2 (over x), score: 16 (over z, y, core).
Axes of the slice: x: 2, y: 2, z: 4, core: 2. Of those that a mesh axis runs over, the one named last changes fastest.
Arguments:
- hidden: bfloat16 [4096, 8192], P(('groups', 'score')), parts along dimension 0, may hold values from -6 to 6
- frozen_query_rows: bfloat16 [4096, 4096], P(('groups', 'score')), parts along dimension 0, may hold values from -64 to 64
- answer_row_key: bfloat16 [4096, 512], P(('groups', 'score')), parts along dimension 0, may hold values from -6 to 6
- answer_row_value: bfloat16 [4096, 512], P(('groups', 'score')), parts along dimension 0, may hold values from -6 to 6
- row_request_index: int32 [4096, 1], P(('groups', 'score')), parts along dimension 0, may hold values from 0 to 15; in each aligned block of 128 rows (0 to 127, 128 to 255, ...) at most 12 rows name the same one
- row_checkpoint_index: int32 [4096], P(('groups', 'score')), parts along dimension 0, may hold values from 0 to 7
- request_device_owner: int32 [32], P('groups'), parts along dimension 0, may hold values from 0 to 15, each once
- request_block_table: int32 [32, 12], P('groups'), parts along dimension 0, may hold values from 0 to 11, each once within a row
- request_prefix_length: int32 [32], P('groups'), parts along dimension 0, may hold values from 128 to 1536
- adapter_down_weight: bfloat16 [8192, 512], P('score'), may hold values from -0.0625 to 0.0625
- adapter_up_weight: bfloat16 [4096, 512], P('score'), may hold values from -0.75 to 0.75
- paged_key_blocks: bfloat16 [384, 128, 512], P(('groups', 'score')), parts along dimension 0, may hold values from -8 to 8
- paged_value_blocks: bfloat16 [384, 128, 512], P(('groups', 'score')), parts along dimension 0, may hold values from -6 to 6
Outputs:
- context: bfloat16 [4096, 4096], P(('groups', 'score')), parts along dimension 0
The draws below stay inside these ranges and needn't reach their ends.
There are 2 independent parts, one for each index of `groups`. The reference program is written for one: setup_inputs(seed, part) draws one part's arguments, and reference() takes and returns one part's arrays. A program takes and returns all parts, laid end to end along the dimension named above; an argument that names none is the same for every part. Nothing has to cross between parts.
Inputs may be any that keep to these rules, and one draw needn't show every extreme that they name: `row_request_index`: among the rows of one device at most 12 name the same request; in some device exactly 12 do. `request_device_owner`: each device stores the prefix of exactly one request. `request_block_table`: each request lists every one of its owner's 12 cache slots once, in prefix order.
All inputs are finite; a program needn't handle non-finite values.
Results may differ from the reference program's by a relative error of at most 0.012.
The reference program's roundings to bfloat16 on the way count: a program that leaves them out, or rounds other values in their place, can miss the bound.
Values may be sent and summed in bfloat16 or wider, within the bound.
A program may use at most 128 MiB of HBM per device.

```python
import math
import jax
import jax.numpy as jnp
import numpy as np
from jax import lax

MODEL_WIDTH = 8192
QUERY_HEADS = 32
KEY_VALUE_HEADS = 4
HEAD_SIZE = 128
ADAPTER_RANK = 64
CHECKPOINT_COUNT = 8
BLOCK_TOKENS = 128
MAXB = 12
ROWS_DEV = 128
QUERY_WIDTH = 4096
KVW = 512
ROWS = 2048
REQS = 16
BLOCK_TOTAL = 192
CAP = 12


def draw_paged_key_blocks(key, part):
    key = jax.random.fold_in(key, 11)
    base_part = jnp.clip(jax.random.normal(key, (BLOCK_TOTAL, BLOCK_TOKENS, KEY_VALUE_HEADS * HEAD_SIZE), jnp.float32), -6.0, 6.0)
    return base_part.astype(jnp.bfloat16)


def draw_frozen_query_rows(key, part):
    key = jax.random.fold_in(key, 12)
    base_part = jnp.clip(jax.random.normal(key, (ROWS, QUERY_HEADS * HEAD_SIZE), jnp.float32), -6.0, 6.0)
    return base_part.astype(jnp.bfloat16)


def with_ends(entries, stream_key, smallest, largest):
    index_at = [jax.random.randint(jax.random.fold_in(stream_key, axis), (), 0, length) for axis, length in enumerate(entries.shape)]
    widest = entries.shape.index(max(entries.shape))
    next_to = index_at[:widest] + [(index_at[widest] + 1) % entries.shape[widest]] + index_at[widest + 1:]
    return entries.at[tuple(index_at)].set(smallest).at[tuple(next_to)].set(largest)


def levels(stream_key, dims, split, smallest, high):
    level = 1.0
    for position, parts in split:
        steps = jax.random.uniform(jax.random.fold_in(jax.random.fold_in(stream_key, 6), position), (parts,), jnp.float32, smallest / len(split), high / len(split))
        level = level * jnp.repeat(jnp.exp(steps), dims[position] // parts).reshape((-1,) + (1,) * (len(dims) - 1 - position))
    return level


def deal_out(key, own, number, rows, count, top, bound, lean):
    ranking = jax.random.permutation(key, count)
    heavy_load, ordinary = shares(count, rows * top, bound, lean, True), shares(count, rows * top, bound, lean, False)
    places = jnp.arange(count)

    def named(sizes, turn):
        used = int((sizes > 0).sum())
        fixed = max(1, used // 4)
        shifted = fixed + (places - fixed + turn * (used - fixed)) % max(1, count - fixed)
        return jnp.zeros((count,), jnp.int32).at[ranking[jnp.where(places < fixed, places, shifted)]].set(jnp.asarray(sizes, jnp.int32))

    sizes = jnp.where(number % 4 == 0, named(heavy_load, number // 4), named(ordinary, number - number // 4 - 1))
    mixed = jax.random.permutation(jax.random.fold_in(own, 3), count)
    giver, sink = mixed[0:count // 2 * 2:2], mixed[1:count // 2 * 2:2]
    margin = jnp.minimum(sizes[giver] - 1, bound - sizes[sink]) // 2
    margin = jnp.where((giver == ranking[0]) | (sink == ranking[0]) | (sizes[sink] == 0), 0, jnp.maximum(margin, 0))
    shifted = jax.random.randint(jax.random.fold_in(own, 4), (count // 2,), 0, 1 << 20) % (margin + 1)
    sizes = sizes.at[giver].add(-shifted).at[sink].add(shifted)
    labels = jnp.searchsorted(jnp.cumsum(sizes), jnp.arange(rows * top), side="right").astype(jnp.int32)
    table = labels.reshape(top, rows).T
    table = table[jax.random.permutation(jax.random.fold_in(own, 1), rows)]
    turn = jax.random.randint(jax.random.fold_in(own, 2), (rows, 1), 0, top)
    return jnp.take_along_axis(table, (jnp.arange(top)[None, :] + turn) % top, axis=1)


def shares(amount, total, limit, skew, full):
    portions = [(1 << 20) // math.isqrt(standing ** skew) + 1 for standing in range(1, amount + 1)]
    largest = limit if full else min(limit, max(-(-total // amount), total * portions[0] // sum(portions)))
    least = 1 if total - largest >= amount - 1 else 0
    holding, surplus = [largest] + [least] * (amount - 1), total - largest - least * (amount - 1)
    while surplus > 0:
        candidates = [i for i in range(1, amount) if holding[i] < largest] or [i for i in range(1, amount) if holding[i] < limit]
        mass, left = sum([portions[i] for i in candidates]), surplus
        for i in candidates:
            addition = min(limit - holding[i], max(1, left * portions[i] // mass), surplus)
            holding[i] = holding[i] + addition
            surplus = surplus - addition
    return np.array(holding)


def bell_draw(rng, shape, spread, limit, cuts=(), held_as=jnp.bfloat16):
    array = spread * jax.random.normal(rng, shape, jnp.float32)
    if cuts:
        array = array * levels(rng, shape, cuts, -0.22, 0.18)
    return jnp.clip(array, -limit, limit).astype(held_as)


def setup_inputs(seed: int = 0, part: int = 0) -> dict:
    streams_of = jax.random.split(jax.random.key(seed), 14)
    own_keys = jax.random.split(jax.random.fold_in(streams_of[13], part), 14)
    hidden = bell_draw(own_keys[0], (ROWS, MODEL_WIDTH), 1.0, 6.0, ((0, 16),))
    frozen_query_rows = draw_frozen_query_rows(jax.random.fold_in(jax.random.fold_in(streams_of[13], part), 71), part)
    answer_row_key = bell_draw(own_keys[2], (ROWS, KVW), 1.0, 6.0, ((0, 16),))
    answer_row_value = bell_draw(own_keys[3], (ROWS, KVW), 1.0, 6.0, ((0, 16),))
    row_request_index_keys = jax.random.split(jax.random.fold_in(own_keys[4], 1), ROWS // ROWS_DEV)
    row_request_index_turns = jax.random.permutation(jax.random.fold_in(own_keys[4], 3), ROWS // ROWS_DEV)
    row_request_index = jax.vmap(lambda own, number: deal_out(jax.random.fold_in(own_keys[4], 2), own, number, ROWS_DEV, REQS, 1, CAP, 2))(row_request_index_keys, row_request_index_turns).reshape((ROWS, 1))
    row_checkpoint_index = with_ends(jax.random.randint(own_keys[5], (ROWS,), 0, CHECKPOINT_COUNT), jax.random.fold_in(own_keys[5], 1), 0, CHECKPOINT_COUNT - 1).astype(jnp.int32)
    request_device_owner = jax.random.permutation(own_keys[6], REQS).astype(jnp.int32)
    request_block_table = jax.vmap(lambda own: jax.random.permutation(own, MAXB))(jax.random.split(own_keys[7], REQS)).reshape((REQS, MAXB)).astype(jnp.int32)
    request_prefix_length = with_ends(jax.random.randint(own_keys[8], (REQS,), BLOCK_TOKENS, MAXB * BLOCK_TOKENS + 1), jax.random.fold_in(own_keys[8], 1), BLOCK_TOKENS, MAXB * BLOCK_TOKENS).astype(jnp.int32)
    adapter_down_weight = bell_draw(streams_of[9], (MODEL_WIDTH, CHECKPOINT_COUNT * ADAPTER_RANK), MODEL_WIDTH ** -0.5, 0.0625, ((0, 16),))
    adapter_up_weight = bell_draw(streams_of[10], (QUERY_WIDTH, CHECKPOINT_COUNT * ADAPTER_RANK), ADAPTER_RANK ** -0.5, 0.75, ((0, 16),))
    paged_key_blocks = draw_paged_key_blocks(jax.random.fold_in(jax.random.fold_in(streams_of[13], part), 71), part)
    paged_value_blocks = bell_draw(own_keys[12], (BLOCK_TOTAL, BLOCK_TOKENS, KVW), 1.0, 6.0, ((0, 16),))
    return {"hidden": hidden, "frozen_query_rows": frozen_query_rows, "answer_row_key": answer_row_key, "answer_row_value": answer_row_value, "row_request_index": row_request_index, "row_checkpoint_index": row_checkpoint_index, "request_device_owner": request_device_owner, "request_block_table": request_block_table, "request_prefix_length": request_prefix_length, "adapter_down_weight": adapter_down_weight, "adapter_up_weight": adapter_up_weight, "paged_key_blocks": paged_key_blocks, "paged_value_blocks": paged_value_blocks}


def rank_projection(hidden, row_checkpoint_index, adapter_down_weight, adapter_up_weight):
    inner_product = jnp.dot(hidden, adapter_down_weight, preferred_element_type=jnp.float32)
    column_owner = jnp.arange(CHECKPOINT_COUNT * ADAPTER_RANK, dtype=jnp.int32) // ADAPTER_RANK
    chosen = row_checkpoint_index[:, None] == column_owner[None, :]
    masked_scores = jnp.where(chosen, inner_product, 0.0).astype(jnp.bfloat16)
    return lax.dot_general(masked_scores, adapter_up_weight, (((1,), (1,)), ((), ())), preferred_element_type=jnp.float32)


def reference(hidden, frozen_query_rows, answer_row_key, answer_row_value, row_request_index, row_checkpoint_index, request_device_owner, request_block_table, request_prefix_length, adapter_down_weight, adapter_up_weight, paged_key_blocks, paged_value_blocks):
    adapter_change = rank_projection(hidden, row_checkpoint_index, adapter_down_weight, adapter_up_weight)
    query = (frozen_query_rows.astype(jnp.float32) + 2.0 * adapter_change).astype(jnp.bfloat16)
    head_group = QUERY_HEADS // KEY_VALUE_HEADS
    token_span = MAXB * BLOCK_TOKENS
    score_scale = 1.0 / (HEAD_SIZE ** 0.5)
    where_blocks = (request_device_owner[:, None] * MAXB + request_block_table).astype(jnp.int32)
    request_key_rows = paged_key_blocks[where_blocks].reshape(REQS, token_span, KVW)
    request_value_rows = paged_value_blocks[where_blocks].reshape(REQS, token_span, KVW)
    block_piece = 64
    item_count = ROWS // block_piece
    requests = row_request_index[:, 0]

    def one_block(items):
        adapted_query_rows, self_key_rows, self_value_rows, request_index = items
        key_rows = request_key_rows[request_index].astype(jnp.float32).reshape(block_piece, token_span, KEY_VALUE_HEADS, HEAD_SIZE)
        value_rows = request_value_rows[request_index].astype(jnp.float32).reshape(block_piece, token_span, KEY_VALUE_HEADS, HEAD_SIZE)
        head_list = adapted_query_rows.astype(jnp.float32).reshape(block_piece, KEY_VALUE_HEADS, head_group, HEAD_SIZE)
        scores = jnp.einsum("phgd,plhd->phgl", head_list, key_rows) * score_scale
        live = jnp.arange(token_span, dtype=jnp.int32)[None, :] < request_prefix_length[request_index][:, None]
        scores = jnp.where(live[:, None, None, :], scores, -jnp.inf)
        own_part = jnp.sum(head_list * self_key_rows.astype(jnp.float32).reshape(block_piece, KEY_VALUE_HEADS, 1, HEAD_SIZE), -1) * score_scale
        top = jnp.maximum(jnp.max(scores, -1), own_part)
        weights = jnp.exp(scores - top[..., None])
        self_weight = jnp.exp(own_part - top)
        total = jnp.sum(weights, -1) + self_weight
        weights = lax.optimization_barrier((weights / total[..., None]).astype(jnp.bfloat16)).astype(jnp.float32)
        self_weight = lax.optimization_barrier((self_weight / total).astype(jnp.bfloat16)).astype(jnp.float32)
        mixed_output = jnp.einsum("phgl,plhd->phgd", weights, value_rows)
        mixed_output = mixed_output + self_weight[..., None] * self_value_rows.astype(jnp.float32).reshape(block_piece, KEY_VALUE_HEADS, 1, HEAD_SIZE)
        return mixed_output.reshape(block_piece, QUERY_WIDTH).astype(jnp.bfloat16)

    result = lax.map(one_block, (query.reshape(item_count, block_piece, QUERY_WIDTH), answer_row_key.reshape(item_count, block_piece, KVW), answer_row_value.reshape(item_count, block_piece, KVW), requests.reshape(item_count, block_piece)))
    return result.reshape(ROWS, QUERY_WIDTH)
```

```python
import functools

import jax
import jax.numpy as jnp
from jax import lax
from jax.experimental import pallas as pl
from jax.experimental.pallas import tpu as pltpu
from jax.sharding import PartitionSpec as P

QUERY_HEADS = 32
KEY_VALUE_HEADS = 4
HEAD_GROUP = QUERY_HEADS // KEY_VALUE_HEADS
HEAD_SIZE = 128
ADAPTER_RANK = 64
BLOCK_TOKENS = 128
MAXB = 12
TOKEN_SPAN = MAXB * BLOCK_TOKENS
SCORE_SCALE = 1.4426950408889634 / HEAD_SIZE**0.5
CHUNK = 256


def attend_kernel(
    frozen_ref, masked_ref, up_ref, key_ref, value_ref, self_key_ref, self_value_ref, bias_ref,
    out_ref, change_ref,
):
    slots = masked_ref.shape[0]
    for head in range(HEAD_GROUP):
        change_ref[pl.ds(head, slots, stride=HEAD_GROUP), :] = lax.dot_general(
            masked_ref[...],
            up_ref[head * HEAD_SIZE : (head + 1) * HEAD_SIZE, :],
            (((1,), (1,)), ((), ())),
            preferred_element_type=jnp.float32,
        )
    keys = key_ref[...].reshape(TOKEN_SPAN, HEAD_SIZE)
    values = value_ref[...].reshape(TOKEN_SPAN, HEAD_SIZE)
    bias = bias_ref[...]

    def spread(rows):
        wide = rows.astype(jnp.float32)[:, None, :]
        return jnp.broadcast_to(wide, (rows.shape[0], HEAD_GROUP, HEAD_SIZE)).reshape(
            rows.shape[0] * HEAD_GROUP, HEAD_SIZE
        )

    for start in range(0, slots * HEAD_GROUP, CHUNK):
        part = slice(start, start + CHUNK)
        part_slots = slice(start // HEAD_GROUP, (start + CHUNK) // HEAD_GROUP)
        query = (frozen_ref[part, :].astype(jnp.float32) + 2.0 * change_ref[part, :]).astype(
            jnp.bfloat16
        )
        scores = (
            lax.dot_general(
                query, keys, (((1,), (1,)), ((), ())), preferred_element_type=jnp.float32
            )
            * SCORE_SCALE
            + bias
        )
        own = (
            jnp.sum(
                query.astype(jnp.float32) * spread(self_key_ref[part_slots, :]), 1, keepdims=True
            )
            * SCORE_SCALE
        )
        top = jnp.maximum(jnp.max(scores, 1, keepdims=True), own)
        weights = jnp.exp2(scores - top)
        self_weight = jnp.exp2(own - top)
        inverse = 1.0 / (jnp.sum(weights, 1, keepdims=True) + self_weight)
        mixed = jnp.dot(
            (weights * inverse).astype(jnp.bfloat16), values, preferred_element_type=jnp.float32
        )
        self_weight = (self_weight * inverse).astype(jnp.bfloat16).astype(jnp.float32)
        out_ref[part, :] = (mixed + self_weight * spread(self_value_ref[part_slots, :])).astype(
            jnp.bfloat16
        )


def attend(frozen, masked, up, keys, values, self_rows, bias):
    slots, columns = masked.shape
    items = slots * HEAD_GROUP
    head_blocks = (MAXB, BLOCK_TOKENS, HEAD_SIZE)
    return pl.pallas_call(
        attend_kernel,
        grid=(KEY_VALUE_HEADS,),
        in_specs=[
            pl.BlockSpec((items, HEAD_SIZE), lambda g: (0, g)),
            pl.BlockSpec((slots, columns), lambda g: (0, 0)),
            pl.BlockSpec((HEAD_GROUP * HEAD_SIZE, columns), lambda g: (g, 0)),
            pl.BlockSpec(head_blocks, lambda g: (0, 0, g)),
            pl.BlockSpec(head_blocks, lambda g: (0, 0, g)),
            pl.BlockSpec((slots, HEAD_SIZE), lambda g: (0, g)),
            pl.BlockSpec((slots, HEAD_SIZE), lambda g: (0, KEY_VALUE_HEADS + g)),
            pl.BlockSpec((1, TOKEN_SPAN), lambda g: (0, 0)),
        ],
        out_specs=pl.BlockSpec((items, HEAD_SIZE), lambda g: (0, g)),
        out_shape=jax.ShapeDtypeStruct((items, KEY_VALUE_HEADS * HEAD_SIZE), jnp.bfloat16),
        scratch_shapes=[pltpu.VMEM((items, HEAD_SIZE), jnp.float32)],
        compiler_params=pltpu.CompilerParams(vmem_limit_bytes=48 * 1024 * 1024),
        name="attend",
    )(frozen, masked, up, keys, values, self_rows, self_rows, bias)


def on_device(
    hidden,
    frozen_query_rows,
    answer_row_key,
    answer_row_value,
    row_request_index,
    row_checkpoint_index,
    request_device_owner,
    request_block_table,
    request_prefix_length,
    adapter_down_weight,
    adapter_up_weight,
    paged_key_blocks,
    paged_value_blocks,
):
    rows = hidden.shape[0]
    devices = lax.axis_size("score")
    capacity = max(2, (3 * rows + 2 * devices - 1) // (2 * devices))
    slots = devices * capacity
    width = frozen_query_rows.shape[1]
    kv_width = answer_row_key.shape[1]
    column_list = adapter_down_weight.shape[1]

    req_ids = jnp.arange(devices, dtype=jnp.int32)
    requests = row_request_index[:, 0]
    picked = requests[:, None] == req_ids[None, :]
    target = jnp.sum(jnp.where(picked, request_device_owner[None, :], 0), 1)
    hits = (target[:, None] == req_ids[None, :]).astype(jnp.int32)
    before = jnp.cumsum(hits, 0) - hits
    slot = target * capacity + jnp.sum(before * hits, 1)
    chooser = (jnp.arange(slots, dtype=jnp.int32)[:, None] == slot[None, :]).astype(jnp.bfloat16)

    def place(value_rows):
        return jnp.dot(chooser, value_rows, preferred_element_type=jnp.float32).astype(
            jnp.bfloat16
        )

    def exchange(filled):
        parts = filled.reshape(devices, filled.shape[0] // devices, filled.shape[1])
        moved = lax.all_to_all(parts, "score", split_axis=0, concat_axis=0, tiled=True)
        return moved.reshape(filled.shape)

    frozen = (
        place(frozen_query_rows)
        .reshape(slots, KEY_VALUE_HEADS, HEAD_GROUP, HEAD_SIZE)
        .transpose(0, 2, 1, 3)
        .reshape(slots * HEAD_GROUP, kv_width)
    )
    frozen = exchange(frozen)
    self_rows = exchange(place(jnp.concatenate([answer_row_key, answer_row_value], 1)))

    down = lax.all_gather(adapter_down_weight, "score", axis=0, tiled=True)
    up = lax.all_gather(adapter_up_weight, "score", axis=0, tiled=True)
    column_owner = jnp.arange(column_list, dtype=jnp.int32) // ADAPTER_RANK
    chosen = row_checkpoint_index[:, None] == column_owner[None, :]
    inner = jnp.dot(hidden, down, preferred_element_type=jnp.float32)
    masked = exchange(place(jnp.where(chosen, inner, 0.0).astype(jnp.bfloat16)))

    here = lax.axis_index("score")
    local_req = jnp.sum(jnp.where(request_device_owner == here, req_ids, 0))
    order = lax.dynamic_index_in_dim(request_block_table, local_req, 0, keepdims=False)
    length = lax.dynamic_index_in_dim(request_prefix_length, local_req, 0, keepdims=False)
    blocks = jnp.arange(MAXB, dtype=jnp.int32)
    place_of = jnp.sum(jnp.where(order[None, :] == blocks[:, None], blocks[None, :], 0), 1)
    position = place_of[:, None] * BLOCK_TOKENS + jnp.arange(BLOCK_TOKENS, dtype=jnp.int32)[None, :]
    bias = jnp.where(position < length, 0.0, -jnp.inf).astype(jnp.float32).reshape(1, TOKEN_SPAN)

    answer = attend(frozen, masked, up, paged_key_blocks, paged_value_blocks, self_rows, bias)
    returned = exchange(answer).reshape(slots, HEAD_GROUP, kv_width)[slot]
    return (
        returned.reshape(rows, HEAD_GROUP, KEY_VALUE_HEADS, HEAD_SIZE)
        .transpose(0, 2, 1, 3)
        .reshape(rows, width)
    )


def solution(mesh):
    placed = (
        P(("groups", "score"), None),
        P(("groups", "score"), None),
        P(("groups", "score"), None),
        P(("groups", "score"), None),
        P(("groups", "score"), None),
        P(("groups", "score")),
        P("groups"),
        P("groups", None),
        P("groups"),
        P("score", None),
        P("score", None),
        P(("groups", "score"), None, None),
        P(("groups", "score"), None, None),
    )
    return jax.shard_map(
        on_device,
        mesh=mesh,
        in_specs=placed,
        out_specs=P(("groups", "score"), None),
        check_vma=False,
    )
```

```python
import functools

import jax
import jax.numpy as jnp
from jax import lax
from jax.experimental import pallas as pl
from jax.experimental.pallas import tpu as pltpu
from jax.sharding import PartitionSpec as P

QUERY_HEADS = 32
KEY_VALUE_HEADS = 4
HEAD_GROUP = QUERY_HEADS // KEY_VALUE_HEADS
HEAD_SIZE = 128
ADAPTER_RANK = 64
BLOCK_TOKENS = 128
MAXB = 12
TOKEN_SPAN = MAXB * BLOCK_TOKENS
SCORE_SCALE = 1.4426950408889634 / HEAD_SIZE**0.5
CHUNK = 256


def attend_kernel(
    frozen_ref, masked_ref, up_ref, key_ref, value_ref, self_key_ref, self_value_ref, bias_ref,
    out_ref, change_ref,
):
    slots = masked_ref.shape[0]
    for head in range(HEAD_GROUP):
        change_ref[pl.ds(head, slots, stride=HEAD_GROUP), :] = lax.dot_general(
            masked_ref[...],
            up_ref[head * HEAD_SIZE : (head + 1) * HEAD_SIZE, :],
            (((1,), (1,)), ((), ())),
            preferred_element_type=jnp.float32,
        )
    keys = key_ref[...].reshape(TOKEN_SPAN, HEAD_SIZE)
    values = value_ref[...].reshape(TOKEN_SPAN, HEAD_SIZE)
    bias = bias_ref[...]

    def spread(rows):
        wide = rows.astype(jnp.float32)[:, None, :]
        return jnp.broadcast_to(wide, (rows.shape[0], HEAD_GROUP, HEAD_SIZE)).reshape(
            rows.shape[0] * HEAD_GROUP, HEAD_SIZE
        )

    for start in range(0, slots * HEAD_GROUP, CHUNK):
        part = slice(start, start + CHUNK)
        part_slots = slice(start // HEAD_GROUP, (start + CHUNK) // HEAD_GROUP)
        query = (frozen_ref[part, :].astype(jnp.float32) + 2.0 * change_ref[part, :]).astype(
            jnp.bfloat16
        )
        scores = (
            lax.dot_general(
                query, keys, (((1,), (1,)), ((), ())), preferred_element_type=jnp.float32
            )
            * SCORE_SCALE
            + bias
        )
        own = (
            jnp.sum(
                query.astype(jnp.float32) * spread(self_key_ref[part_slots, :]), 1, keepdims=True
            )
            * SCORE_SCALE
        )
        top = jnp.maximum(jnp.max(scores, 1, keepdims=True), own)
        weights = jnp.exp2(scores - top)
        self_weight = jnp.exp2(own - top)
        inverse = 1.0 / (jnp.sum(weights, 1, keepdims=True) + self_weight)
        mixed = jnp.dot(
            (weights * inverse).astype(jnp.bfloat16), values, preferred_element_type=jnp.float32
        )
        self_weight = (self_weight * inverse).astype(jnp.bfloat16).astype(jnp.float32)
        out_ref[part, :] = (mixed + self_weight * spread(self_value_ref[part_slots, :])).astype(
            jnp.bfloat16
        )


def attend(frozen, masked, up, keys, values, self_rows, bias):
    slots, columns = masked.shape
    items = slots * HEAD_GROUP
    head_blocks = (MAXB, BLOCK_TOKENS, HEAD_SIZE)
    return pl.pallas_call(
        attend_kernel,
        grid=(KEY_VALUE_HEADS,),
        in_specs=[
            pl.BlockSpec((items, HEAD_SIZE), lambda g: (0, g)),
            pl.BlockSpec((slots, columns), lambda g: (0, 0)),
            pl.BlockSpec((HEAD_GROUP * HEAD_SIZE, columns), lambda g: (g, 0)),
            pl.BlockSpec(head_blocks, lambda g: (0, 0, g)),
            pl.BlockSpec(head_blocks, lambda g: (0, 0, g)),
            pl.BlockSpec((slots, HEAD_SIZE), lambda g: (0, g)),
            pl.BlockSpec((slots, HEAD_SIZE), lambda g: (0, KEY_VALUE_HEADS + g)),
            pl.BlockSpec((1, TOKEN_SPAN), lambda g: (0, 0)),
        ],
        out_specs=pl.BlockSpec((items, HEAD_SIZE), lambda g: (0, g)),
        out_shape=jax.ShapeDtypeStruct((items, KEY_VALUE_HEADS * HEAD_SIZE), jnp.bfloat16),
        scratch_shapes=[pltpu.VMEM((items, HEAD_SIZE), jnp.float32)],
        compiler_params=pltpu.CompilerParams(vmem_limit_bytes=48 * 1024 * 1024),
        name="attend",
    )(frozen, masked, up, keys, values, self_rows, self_rows, bias)


def ring_chip(place, chips):
    half = chips // 2
    side = lax.div(place, half)
    step = lax.rem(place, half)
    return 2 * (step * (1 - side) + (half - 1 - step) * side) + side


def feed_kernel(
    devices, hidden_ref, chosen_ref, chooser_ref, down_ref, up_ref, frozen_ref, self_ref,
    up_full, frozen_out, self_out, masked_out,
    down_full, total, masked_send, pieces, row_sems, local_sems,
):
    chips = devices // 2
    group = lax.axis_index("groups")
    here = lax.axis_index("score")
    chip, core = lax.div(here, 2), lax.rem(here, 2)
    step_of, side = lax.div(chip, 2), lax.rem(chip, 2)
    place = side * (chips - 1 - step_of) + (1 - side) * step_of
    after = ring_chip(lax.rem(place + 1, chips), chips) * 2 + core
    before = ring_chip(lax.rem(place + chips - 1, chips), chips) * 2 + core
    sibling = chip * 2 + 1 - core
    next_on = (after, before)
    sources = (down_ref, up_ref)
    fulls = (down_full, up_full)
    parts = HEAD_SIZE

    barrier = pltpu.get_barrier_semaphore()

    @pl.loop(1, devices)
    def _(offset):
        pl.semaphore_signal(
            barrier, inc=1, device_id={"score": lax.rem(here + offset, devices)},
            device_id_type=pl.DeviceIdType.MESH,
        )

    pl.semaphore_signal(
        barrier, inc=1, device_id={"groups": 1 - group}, device_id_type=pl.DeviceIdType.MESH
    )
    pl.semaphore_wait(barrier, devices)

    def remote(source, target, send, recv, device):
        return pltpu.make_async_remote_copy(
            src_ref=source, dst_ref=target, send_sem=send, recv_sem=recv, device_id=device,
            device_id_type=pl.DeviceIdType.MESH,
        )

    def shard(a, owner, quarter=None):
        rows = sources[a].shape[0]
        span = pl.ds(pl.multiple_of(owner * rows, rows), rows)
        if quarter is None:
            return fulls[a].at[span, :]
        return fulls[a].at[span, pl.ds(pl.multiple_of(quarter * parts, parts), parts)]

    def origin(d, t):
        turn = place + chips - t if d == 0 else place + t
        return ring_chip(lax.rem(turn, chips), chips)

    def ring(a, d, t):
        ref = shard(a, origin(d, t) * 2 + core, group * 2 + d)
        return remote(ref, ref, pieces.at[0, a, d, t], pieces.at[1, a, d, t], {"score": next_on[d]})

    def beside(a, d, t):
        ref = shard(a, origin(d, t) * 2 + core, group * 2 + d)
        return remote(ref, ref, pieces.at[2, a, d, t], pieces.at[3, a, d, t], {"score": sibling})

    def across(a, d, t):
        ref = shard(a, origin(d, t) * 2 + core, group * 2 + d)
        return remote(ref, ref, pieces.at[4, a, d, t], pieces.at[5, a, d, t], {"groups": 1 - group})

    def onward(a, d, t):
        ref = shard(a, origin(d, t) * 2 + core, (1 - group) * 2 + d)
        return remote(ref, ref, pieces.at[6, a, d, t], pieces.at[7, a, d, t], {"score": sibling})

    def whole(a):
        ref = shard(a, here)
        return remote(ref, ref, pieces.at[2, a, 0, 0], pieces.at[3, a, 0, 0], {"score": sibling})

    def rows_to(kind, offset):
        peer = lax.rem(here + offset, devices)
        source = (frozen_ref, self_ref, masked_send)[kind]
        target = (frozen_out, self_out, masked_out)[kind]
        size = source.shape[0] // devices
        return remote(
            source.at[pl.ds(pl.multiple_of(peer * size, size), size), :],
            target.at[pl.ds(pl.multiple_of(here * size, size), size), :],
            row_sems.at[0, kind, offset],
            row_sems.at[1, kind, offset],
            {"score": peer},
        )

    def rows_here(kind):
        source = (frozen_ref, self_ref, masked_send)[kind]
        target = (frozen_out, self_out, masked_out)[kind]
        size = source.shape[0] // devices
        span = pl.ds(pl.multiple_of(here * size, size), size)
        return pltpu.make_async_copy(source.at[span, :], target.at[span, :], local_sems.at[2 + kind])

    own = [pltpu.make_async_copy(sources[a], shard(a, here), local_sems.at[a]) for a in range(2)]
    for copy in own:
        copy.start()
    rows_here(0).start()
    rows_here(1).start()
    for copy in own:
        copy.wait()

    def begin(a):
        for d in range(2):
            ring(a, d, 0).start()
        whole(a).start()

    def circle(a):
        @pl.loop(0, chips - 1)
        def _(t):
            for d in range(2):
                ring(a, d, t).wait_recv()

                @pl.when(t < chips - 2)
                def _():
                    ring(a, d, t + 1).start()

                across(a, d, t + 1).start()
                beside(a, d, t + 1).start()
            if a == 0:
                for extra in range(2):
                    rows_to(0, 2 * t + 1 + extra).start()
                    rows_to(1, 2 * t + 1 + extra).start()

            @pl.when(t > 0)
            def _():
                for d in range(2):
                    across(a, d, t).wait_recv()
                    onward(a, d, t).start()

    def finish(a):
        for d in range(2):
            across(a, d, chips - 1).wait_recv()
            onward(a, d, chips - 1).start()
        whole(a).wait_recv()

        @pl.loop(1, chips)
        def _(t):
            for d in range(2):
                beside(a, d, t).wait_recv()
                onward(a, d, t).wait_recv()

    begin(0)
    rows_to(0, devices - 1).start()
    rows_to(1, devices - 1).start()
    circle(0)
    begin(1)
    finish(0)

    total[...] = jnp.zeros_like(total)
    depth = hidden_ref.shape[1] // 8

    @pl.loop(0, 8)
    def _(k):
        span = pl.ds(pl.multiple_of(k * depth, depth), depth)
        total[...] += jnp.dot(
            hidden_ref[:, span], down_full[span, :], preferred_element_type=jnp.float32
        )

    masked = jnp.where(chosen_ref[...] != 0, total[...], 0.0).astype(jnp.bfloat16)
    masked_send[...] = jnp.dot(
        chooser_ref[...], masked, preferred_element_type=jnp.float32
    ).astype(jnp.bfloat16)
    rows_here(2).start()

    @pl.loop(1, devices)
    def _(offset):
        rows_to(2, offset).start()

    circle(1)
    finish(1)

    for kind in range(3):
        rows_here(kind).wait()

    @pl.loop(1, devices)
    def _(offset):
        for kind in range(3):
            rows_to(kind, offset).wait()

    for a in range(2):
        whole(a).wait_send()
        for d in range(2):
            ring(a, d, 0).wait_send()

        @pl.loop(1, chips)
        def _(t):
            for d in range(2):
                @pl.when(t < chips - 1)
                def _():
                    ring(a, d, t).wait_send()

                beside(a, d, t).wait_send()
                across(a, d, t).wait_send()
                onward(a, d, t).wait_send()


def feed(devices, hidden, chosen, chooser, down, up, frozen, self_rows):
    rows, columns = chosen.shape
    padded = chooser.shape[0]
    vmem, anywhere = pl.BlockSpec(memory_space=pltpu.VMEM), pl.BlockSpec(memory_space=pl.ANY)
    shape = lambda *dims: jax.ShapeDtypeStruct(dims, jnp.bfloat16)
    return pl.pallas_call(
        functools.partial(feed_kernel, devices),
        in_specs=[vmem, vmem, vmem, anywhere, anywhere, anywhere, anywhere],
        out_specs=[anywhere] * 4,
        out_shape=[
            shape(up.shape[0] * devices, columns),
            shape(*frozen.shape),
            shape(*self_rows.shape),
            shape(padded, columns),
        ],
        scratch_shapes=[
            pltpu.VMEM((down.shape[0] * devices, columns), jnp.bfloat16),
            pltpu.VMEM((rows, columns), jnp.float32),
            pltpu.VMEM((padded, columns), jnp.bfloat16),
            pltpu.SemaphoreType.DMA((8, 2, 2, devices // 2)),
            pltpu.SemaphoreType.DMA((2, 3, devices)),
            pltpu.SemaphoreType.DMA((5,)),
        ],
        compiler_params=pltpu.CompilerParams(
            collective_id=0, has_side_effects=True, vmem_limit_bytes=40 * 1024 * 1024
        ),
        name="feed",
    )(hidden, chosen, chooser, down, up, frozen, self_rows)


def on_device(
    hidden,
    frozen_query_rows,
    answer_row_key,
    answer_row_value,
    row_request_index,
    row_checkpoint_index,
    request_device_owner,
    request_block_table,
    request_prefix_length,
    adapter_down_weight,
    adapter_up_weight,
    paged_key_blocks,
    paged_value_blocks,
):
    rows = hidden.shape[0]
    devices = lax.axis_size("score")
    capacity = max(2, (3 * rows + 2 * devices - 1) // (2 * devices))
    slots = devices * capacity
    width = frozen_query_rows.shape[1]
    kv_width = answer_row_key.shape[1]
    column_list = adapter_down_weight.shape[1]

    req_ids = jnp.arange(devices, dtype=jnp.int32)
    requests = row_request_index[:, 0]
    picked = requests[:, None] == req_ids[None, :]
    target = jnp.sum(jnp.where(picked, request_device_owner[None, :], 0), 1)
    hits = (target[:, None] == req_ids[None, :]).astype(jnp.int32)
    before = jnp.cumsum(hits, 0) - hits
    slot = target * capacity + jnp.sum(before * hits, 1)
    chooser = (jnp.arange(slots, dtype=jnp.int32)[:, None] == slot[None, :]).astype(jnp.bfloat16)

    def place(value_rows):
        return jnp.dot(chooser, value_rows, preferred_element_type=jnp.float32).astype(
            jnp.bfloat16
        )

    def exchange(filled):
        parts = filled.reshape(devices, filled.shape[0] // devices, filled.shape[1])
        moved = lax.all_to_all(parts, "score", split_axis=0, concat_axis=0, tiled=True)
        return moved.reshape(filled.shape)

    frozen = (
        place(frozen_query_rows)
        .reshape(slots, KEY_VALUE_HEADS, HEAD_GROUP, HEAD_SIZE)
        .transpose(0, 2, 1, 3)
        .reshape(slots * HEAD_GROUP, kv_width)
    )
    pitch = -(-capacity // 16) * 16
    wide_slot = slot // capacity * pitch + slot % capacity
    wide_ids = jnp.arange(devices * pitch, dtype=jnp.int32)
    wide = (wide_ids[:, None] == wide_slot[None, :]).astype(jnp.bfloat16)
    self_rows = jnp.dot(
        wide,
        jnp.concatenate([answer_row_key, answer_row_value], 1),
        preferred_element_type=jnp.float32,
    ).astype(jnp.bfloat16)
    column_owner = jnp.arange(column_list, dtype=jnp.int32) // ADAPTER_RANK
    chosen = (row_checkpoint_index[:, None] == column_owner[None, :]).astype(jnp.float32)
    up, frozen, self_rows, masked = feed(
        devices, hidden, chosen, wide, adapter_down_weight, adapter_up_weight, frozen, self_rows
    )

    def tight(spaced):
        parts = spaced.reshape(devices, pitch, spaced.shape[1])[:, :capacity]
        return parts.reshape(slots, spaced.shape[1])

    self_rows, masked = tight(self_rows), tight(masked)

    here = lax.axis_index("score")
    local_req = jnp.sum(jnp.where(request_device_owner == here, req_ids, 0))
    order = lax.dynamic_index_in_dim(request_block_table, local_req, 0, keepdims=False)
    length = lax.dynamic_index_in_dim(request_prefix_length, local_req, 0, keepdims=False)
    blocks = jnp.arange(MAXB, dtype=jnp.int32)
    place_of = jnp.sum(jnp.where(order[None, :] == blocks[:, None], blocks[None, :], 0), 1)
    position = place_of[:, None] * BLOCK_TOKENS + jnp.arange(BLOCK_TOKENS, dtype=jnp.int32)[None, :]
    bias = jnp.where(position < length, 0.0, -jnp.inf).astype(jnp.float32).reshape(1, TOKEN_SPAN)

    answer = attend(frozen, masked, up, paged_key_blocks, paged_value_blocks, self_rows, bias)
    returned = exchange(answer).reshape(slots, HEAD_GROUP, kv_width)[slot]
    return (
        returned.reshape(rows, HEAD_GROUP, KEY_VALUE_HEADS, HEAD_SIZE)
        .transpose(0, 2, 1, 3)
        .reshape(rows, width)
    )


def solution(mesh):
    placed = (
        P(("groups", "score"), None),
        P(("groups", "score"), None),
        P(("groups", "score"), None),
        P(("groups", "score"), None),
        P(("groups", "score"), None),
        P(("groups", "score")),
        P("groups"),
        P("groups", None),
        P("groups"),
        P("score", None),
        P("score", None),
        P(("groups", "score"), None, None),
        P(("groups", "score"), None, None),
    )
    return jax.shard_map(
        on_device,
        mesh=mesh,
        in_specs=placed,
        out_specs=P(("groups", "score"), None),
        check_vma=False,
    )
```

```python
import functools

import jax
import jax.numpy as jnp
from jax import lax
from jax.experimental import pallas as pl
from jax.experimental.pallas import tpu as pltpu
from jax.sharding import PartitionSpec as P

QUERY_HEADS = 32
KEY_VALUE_HEADS = 4
HEAD_GROUP = QUERY_HEADS // KEY_VALUE_HEADS
HEAD_SIZE = 128
ADAPTER_RANK = 64
BLOCK_TOKENS = 128
MAXB = 12
TOKEN_SPAN = MAXB * BLOCK_TOKENS
SCORE_SCALE = 1.4426950408889634 / HEAD_SIZE**0.5
CHUNK = 256
LAG = 2
PEERS = 1


def attend_kernel(
    frozen_ref, masked_ref, up_ref, key_ref, value_ref, self_key_ref, self_value_ref, bias_ref,
    out_ref, change_ref,
):
    slots = masked_ref.shape[0]
    for head in range(HEAD_GROUP):
        change_ref[pl.ds(head, slots, stride=HEAD_GROUP), :] = lax.dot_general(
            masked_ref[...],
            up_ref[head * HEAD_SIZE : (head + 1) * HEAD_SIZE, :],
            (((1,), (1,)), ((), ())),
            preferred_element_type=jnp.float32,
        )
    keys = key_ref[...].reshape(TOKEN_SPAN, HEAD_SIZE)
    values = value_ref[...].reshape(TOKEN_SPAN, HEAD_SIZE)
    bias = bias_ref[...]

    def spread(rows):
        wide = rows.astype(jnp.float32)[:, None, :]
        return jnp.broadcast_to(wide, (rows.shape[0], HEAD_GROUP, HEAD_SIZE)).reshape(
            rows.shape[0] * HEAD_GROUP, HEAD_SIZE
        )

    for start in range(0, slots * HEAD_GROUP, CHUNK):
        part = slice(start, start + CHUNK)
        part_slots = slice(start // HEAD_GROUP, (start + CHUNK) // HEAD_GROUP)
        query = (frozen_ref[part, :].astype(jnp.float32) + 2.0 * change_ref[part, :]).astype(
            jnp.bfloat16
        )
        scores = (
            lax.dot_general(
                query, keys, (((1,), (1,)), ((), ())), preferred_element_type=jnp.float32
            )
            * SCORE_SCALE
            + bias
        )
        own = (
            jnp.sum(
                query.astype(jnp.float32) * spread(self_key_ref[part_slots, :]), 1, keepdims=True
            )
            * SCORE_SCALE
        )
        top = jnp.maximum(jnp.max(scores, 1, keepdims=True), own)
        weights = jnp.exp2(scores - top)
        self_weight = jnp.exp2(own - top)
        inverse = 1.0 / (jnp.sum(weights, 1, keepdims=True) + self_weight)
        mixed = jnp.dot(
            (weights * inverse).astype(jnp.bfloat16), values, preferred_element_type=jnp.float32
        )
        self_weight = (self_weight * inverse).astype(jnp.bfloat16).astype(jnp.float32)
        out_ref[part, :] = (mixed + self_weight * spread(self_value_ref[part_slots, :])).astype(
            jnp.bfloat16
        )


def attend(frozen, masked, up, keys, values, self_rows, bias):
    slots, columns = masked.shape
    items = slots * HEAD_GROUP
    head_blocks = (MAXB, BLOCK_TOKENS, HEAD_SIZE)
    return pl.pallas_call(
        attend_kernel,
        grid=(KEY_VALUE_HEADS,),
        in_specs=[
            pl.BlockSpec((items, HEAD_SIZE), lambda g: (0, g)),
            pl.BlockSpec((slots, columns), lambda g: (0, 0)),
            pl.BlockSpec((HEAD_GROUP * HEAD_SIZE, columns), lambda g: (g, 0)),
            pl.BlockSpec(head_blocks, lambda g: (0, 0, g)),
            pl.BlockSpec(head_blocks, lambda g: (0, 0, g)),
            pl.BlockSpec((slots, HEAD_SIZE), lambda g: (0, g)),
            pl.BlockSpec((slots, HEAD_SIZE), lambda g: (0, KEY_VALUE_HEADS + g)),
            pl.BlockSpec((1, TOKEN_SPAN), lambda g: (0, 0)),
        ],
        out_specs=pl.BlockSpec((items, HEAD_SIZE), lambda g: (0, g)),
        out_shape=jax.ShapeDtypeStruct((items, KEY_VALUE_HEADS * HEAD_SIZE), jnp.bfloat16),
        scratch_shapes=[pltpu.VMEM((items, HEAD_SIZE), jnp.float32)],
        compiler_params=pltpu.CompilerParams(vmem_limit_bytes=48 * 1024 * 1024),
        name="attend",
    )(frozen, masked, up, keys, values, self_rows, self_rows, bias)


def ring_chip(place, chips):
    half = chips // 2
    side = lax.div(place, half)
    step = lax.rem(place, half)
    return 2 * (step * (1 - side) + (half - 1 - step) * side) + side


def feed_kernel(
    devices, hidden_ref, chosen_ref, chooser_ref, down_ref, up_ref, frozen_ref, self_ref,
    up_full, frozen_out, self_out, masked_out,
    down_full, total, masked_send, pieces, row_sems, local_sems,
):
    chips = devices // 2
    group = lax.axis_index("groups")
    here = lax.axis_index("score")
    chip, core = lax.div(here, 2), lax.rem(here, 2)
    step_of, side = lax.div(chip, 2), lax.rem(chip, 2)
    place = side * (chips - 1 - step_of) + (1 - side) * step_of
    after = ring_chip(lax.rem(place + 1, chips), chips) * 2 + core
    before = ring_chip(lax.rem(place + chips - 1, chips), chips) * 2 + core
    sibling = chip * 2 + 1 - core
    next_on = (after, before)
    sources = (down_ref, up_ref)
    fulls = (down_full, up_full)
    parts = HEAD_SIZE

    barrier = pltpu.get_barrier_semaphore()

    @pl.loop(1, devices)
    def _(offset):
        pl.semaphore_signal(
            barrier, inc=1, device_id={"score": lax.rem(here + offset, devices)},
            device_id_type=pl.DeviceIdType.MESH,
        )

    pl.semaphore_signal(
        barrier, inc=1, device_id={"groups": 1 - group}, device_id_type=pl.DeviceIdType.MESH
    )
    pl.semaphore_wait(barrier, devices)

    def remote(source, target, send, recv, device):
        return pltpu.make_async_remote_copy(
            src_ref=source, dst_ref=target, send_sem=send, recv_sem=recv, device_id=device,
            device_id_type=pl.DeviceIdType.MESH,
        )

    def shard(a, owner, quarter=None):
        rows = sources[a].shape[0]
        span = pl.ds(pl.multiple_of(owner * rows, rows), rows)
        if quarter is None:
            return fulls[a].at[span, :]
        if rows % 64 == 0:
            size = rows // 4
            first = pl.multiple_of(owner * rows + quarter * size, size)
            return fulls[a].at[pl.ds(first, size), :]
        return fulls[a].at[span, pl.ds(pl.multiple_of(quarter * parts, parts), parts)]

    def origin(d, t):
        turn = place + chips - t if d == 0 else place + t
        return ring_chip(lax.rem(turn, chips), chips)

    def ring(a, d, t):
        ref = shard(a, origin(d, t) * 2 + core, group * 2 + d)
        return remote(ref, ref, pieces.at[0, a, d, t], pieces.at[1, a, d, t], {"score": next_on[d]})

    def beside(a, d, t):
        ref = shard(a, origin(d, t) * 2 + core, group * 2 + d)
        return remote(ref, ref, pieces.at[2, a, d, t], pieces.at[3, a, d, t], {"score": sibling})

    def across(a, d, t):
        ref = shard(a, origin(d, t) * 2 + core, group * 2 + d)
        return remote(ref, ref, pieces.at[4, a, d, t], pieces.at[5, a, d, t], {"groups": 1 - group})

    def onward(a, d, t):
        ref = shard(a, origin(d, t) * 2 + core, (1 - group) * 2 + d)
        return remote(ref, ref, pieces.at[6, a, d, t], pieces.at[7, a, d, t], {"score": sibling})

    def whole(a):
        ref = shard(a, here)
        return remote(ref, ref, pieces.at[2, a, 0, 0], pieces.at[3, a, 0, 0], {"score": sibling})

    def rows_to(kind, offset):
        peer = lax.rem(here + offset, devices)
        source = (frozen_ref, self_ref, masked_send)[kind]
        target = (frozen_out, self_out, masked_out)[kind]
        size = source.shape[0] // devices
        return remote(
            source.at[pl.ds(pl.multiple_of(peer * size, size), size), :],
            target.at[pl.ds(pl.multiple_of(here * size, size), size), :],
            row_sems.at[0, kind, offset],
            row_sems.at[1, kind, offset],
            {"score": peer},
        )

    def rows_here(kind):
        source = (frozen_ref, self_ref, masked_send)[kind]
        target = (frozen_out, self_out, masked_out)[kind]
        size = source.shape[0] // devices
        span = pl.ds(pl.multiple_of(here * size, size), size)
        return pltpu.make_async_copy(source.at[span, :], target.at[span, :], local_sems.at[2 + kind])

    own = [pltpu.make_async_copy(sources[a], shard(a, here), local_sems.at[a]) for a in range(2)]
    for copy in own:
        copy.start()
    rows_here(0).start()
    rows_here(1).start()
    for copy in own:
        copy.wait()

    def begin(a):
        for d in range(2):
            ring(a, d, 0).start()
        whole(a).start()

    def step(a, t):
        for d in range(2):
            ring(a, d, t).wait_recv()

            @pl.when(t < chips - 2)
            def _():
                ring(a, d, t + 1).start()

            across(a, d, t + 1).start()
            beside(a, d, t + 1).start()

        @pl.when(t > 0)
        def _():
            for d in range(2):
                across(a, d, t).wait_recv()
                onward(a, d, t).start()

    def send_rows(turn):
        offset = lax.rem(turn + devices // 2 - 1, devices - 1) + 1
        rows_to(0, offset).start()
        rows_to(1, offset).start()

    def finish(a):
        for d in range(2):
            across(a, d, chips - 1).wait_recv()
            onward(a, d, chips - 1).start()
        whole(a).wait_recv()

        @pl.loop(1, chips)
        def _(t):
            for d in range(2):
                beside(a, d, t).wait_recv()
                onward(a, d, t).wait_recv()

    begin(0)
    begin(1)
    lag = min(LAG, chips - 1)

    @pl.loop(0, chips - 1)
    def _(t):
        step(0, t)

        @pl.when(t >= lag)
        def _():
            step(1, t - lag)

        for extra in range(PEERS):
            send_rows(PEERS * t + extra)

    @pl.loop(PEERS * (chips - 1), devices - 1)
    def _(turn):
        send_rows(turn)

    finish(0)

    total[...] = jnp.zeros_like(total)
    depth = hidden_ref.shape[1] // 8

    @pl.loop(0, 8)
    def _(k):
        span = pl.ds(pl.multiple_of(k * depth, depth), depth)
        total[...] += jnp.dot(
            hidden_ref[:, span], down_full[span, :], preferred_element_type=jnp.float32
        )

    masked = jnp.where(chosen_ref[...] != 0, total[...], 0.0).astype(jnp.bfloat16)
    masked_send[...] = jnp.dot(
        chooser_ref[...], masked, preferred_element_type=jnp.float32
    ).astype(jnp.bfloat16)
    rows_here(2).start()

    @pl.loop(1, devices)
    def _(offset):
        rows_to(2, offset).start()

    @pl.loop(chips - 1 - lag, chips - 1)
    def _(t):
        step(1, t)

    finish(1)

    for kind in range(3):
        rows_here(kind).wait()

    @pl.loop(1, devices)
    def _(offset):
        for kind in range(3):
            rows_to(kind, offset).wait()

    for a in range(2):
        whole(a).wait_send()
        for d in range(2):
            ring(a, d, 0).wait_send()

        @pl.loop(1, chips)
        def _(t):
            for d in range(2):
                @pl.when(t < chips - 1)
                def _():
                    ring(a, d, t).wait_send()

                beside(a, d, t).wait_send()
                across(a, d, t).wait_send()
                onward(a, d, t).wait_send()


def feed(devices, hidden, chosen, chooser, down, up, frozen, self_rows):
    rows, columns = chosen.shape
    padded = chooser.shape[0]
    vmem, anywhere = pl.BlockSpec(memory_space=pltpu.VMEM), pl.BlockSpec(memory_space=pl.ANY)
    shape = lambda *dims: jax.ShapeDtypeStruct(dims, jnp.bfloat16)
    return pl.pallas_call(
        functools.partial(feed_kernel, devices),
        in_specs=[vmem, vmem, vmem, anywhere, anywhere, anywhere, anywhere],
        out_specs=[anywhere] * 4,
        out_shape=[
            shape(up.shape[0] * devices, columns),
            shape(*frozen.shape),
            shape(*self_rows.shape),
            shape(padded, columns),
        ],
        scratch_shapes=[
            pltpu.VMEM((down.shape[0] * devices, columns), jnp.bfloat16),
            pltpu.VMEM((rows, columns), jnp.float32),
            pltpu.VMEM((padded, columns), jnp.bfloat16),
            pltpu.SemaphoreType.DMA((8, 2, 2, devices // 2)),
            pltpu.SemaphoreType.DMA((2, 3, devices)),
            pltpu.SemaphoreType.DMA((5,)),
        ],
        compiler_params=pltpu.CompilerParams(
            collective_id=0, has_side_effects=True, vmem_limit_bytes=40 * 1024 * 1024
        ),
        name="feed",
    )(hidden, chosen, chooser, down, up, frozen, self_rows)


def on_device(
    hidden,
    frozen_query_rows,
    answer_row_key,
    answer_row_value,
    row_request_index,
    row_checkpoint_index,
    request_device_owner,
    request_block_table,
    request_prefix_length,
    adapter_down_weight,
    adapter_up_weight,
    paged_key_blocks,
    paged_value_blocks,
):
    rows = hidden.shape[0]
    devices = lax.axis_size("score")
    capacity = max(2, (3 * rows + 2 * devices - 1) // (2 * devices))
    slots = devices * capacity
    width = frozen_query_rows.shape[1]
    kv_width = answer_row_key.shape[1]
    column_list = adapter_down_weight.shape[1]

    req_ids = jnp.arange(devices, dtype=jnp.int32)
    requests = row_request_index[:, 0]
    picked = requests[:, None] == req_ids[None, :]
    target = jnp.sum(jnp.where(picked, request_device_owner[None, :], 0), 1)
    hits = (target[:, None] == req_ids[None, :]).astype(jnp.int32)
    before = jnp.cumsum(hits, 0) - hits
    slot = target * capacity + jnp.sum(before * hits, 1)
    chooser = (jnp.arange(slots, dtype=jnp.int32)[:, None] == slot[None, :]).astype(jnp.bfloat16)

    def place(value_rows):
        return jnp.dot(chooser, value_rows, preferred_element_type=jnp.float32).astype(
            jnp.bfloat16
        )

    def exchange(filled):
        parts = filled.reshape(devices, filled.shape[0] // devices, filled.shape[1])
        moved = lax.all_to_all(parts, "score", split_axis=0, concat_axis=0, tiled=True)
        return moved.reshape(filled.shape)

    frozen = (
        place(frozen_query_rows)
        .reshape(slots, KEY_VALUE_HEADS, HEAD_GROUP, HEAD_SIZE)
        .transpose(0, 2, 1, 3)
        .reshape(slots * HEAD_GROUP, kv_width)
    )
    pitch = -(-capacity // 16) * 16
    wide_slot = slot // capacity * pitch + slot % capacity
    wide_ids = jnp.arange(devices * pitch, dtype=jnp.int32)
    wide = (wide_ids[:, None] == wide_slot[None, :]).astype(jnp.bfloat16)
    self_rows = place(jnp.concatenate([answer_row_key, answer_row_value], 1)).reshape(
        slots * 2 * KEY_VALUE_HEADS, HEAD_SIZE
    )
    column_owner = jnp.arange(column_list, dtype=jnp.int32) // ADAPTER_RANK
    chosen = (row_checkpoint_index[:, None] == column_owner[None, :]).astype(jnp.float32)
    here = lax.axis_index("score")
    local_req = jnp.sum(jnp.where(request_device_owner == here, req_ids, 0))
    order = lax.dynamic_index_in_dim(request_block_table, local_req, 0, keepdims=False)
    length = lax.dynamic_index_in_dim(request_prefix_length, local_req, 0, keepdims=False)
    blocks = jnp.arange(MAXB, dtype=jnp.int32)
    place_of = jnp.sum(jnp.where(order[None, :] == blocks[:, None], blocks[None, :], 0), 1)
    position = place_of[:, None] * BLOCK_TOKENS + jnp.arange(BLOCK_TOKENS, dtype=jnp.int32)[None, :]
    bias = jnp.where(position < length, 0.0, -jnp.inf).astype(jnp.float32).reshape(1, TOKEN_SPAN)

    frozen, bias = lax.optimization_barrier((frozen, bias))
    up, frozen, self_rows, masked = feed(
        devices, hidden, chosen, wide, adapter_down_weight, adapter_up_weight, frozen, self_rows
    )

    self_rows = self_rows.reshape(slots, 2 * kv_width)
    masked = masked.reshape(devices, pitch, column_list)[:, :capacity].reshape(slots, column_list)

    answer = attend(frozen, masked, up, paged_key_blocks, paged_value_blocks, self_rows, bias)
    returned = exchange(answer).reshape(slots, HEAD_GROUP, kv_width)[slot]
    return (
        returned.reshape(rows, HEAD_GROUP, KEY_VALUE_HEADS, HEAD_SIZE)
        .transpose(0, 2, 1, 3)
        .reshape(rows, width)
    )


def solution(mesh):
    placed = (
        P(("groups", "score"), None),
        P(("groups", "score"), None),
        P(("groups", "score"), None),
        P(("groups", "score"), None),
        P(("groups", "score"), None),
        P(("groups", "score")),
        P("groups"),
        P("groups", None),
        P("groups"),
        P("score", None),
        P("score", None),
        P(("groups", "score"), None, None),
        P(("groups", "score"), None, None),
    )
    return jax.shard_map(
        on_device,
        mesh=mesh,
        in_specs=placed,
        out_specs=P(("groups", "score"), None),
        check_vma=False,
    )
```

```python
import functools

import jax
import jax.numpy as jnp
from jax import lax
from jax.experimental import pallas as pl
from jax.experimental.pallas import tpu as pltpu
from jax.sharding import PartitionSpec as P

QUERY_HEADS = 32
KEY_VALUE_HEADS = 4
HEAD_GROUP = QUERY_HEADS // KEY_VALUE_HEADS
HEAD_SIZE = 128
ADAPTER_RANK = 64
BLOCK_TOKENS = 128
MAXB = 12
TOKEN_SPAN = MAXB * BLOCK_TOKENS
SCORE_SCALE = 1.4426950408889634 / HEAD_SIZE**0.5
CHUNK = 256
LAG = 2
PEERS = 1


def attend_kernel(
    devices, frozen_ref, masked_ref, up_ref, key_ref, value_ref, self_key_ref, self_value_ref, bias_ref,
    out_ref, change_ref, answer_ref, sems, local_sems,
):
    slots = masked_ref.shape[0]
    share = slots * HEAD_GROUP // devices
    here = lax.axis_index("score")
    turn = pl.program_id(0)
    barrier = pltpu.get_barrier_semaphore()

    @pl.when(turn == 0)
    def _():
        @pl.loop(1, devices)
        def _(offset):
            pl.semaphore_signal(
                barrier, inc=1, device_id={"score": lax.rem(here + offset, devices)},
                device_id_type=pl.DeviceIdType.MESH,
            )

    def back(g, offset):
        peer = lax.rem(here + offset, devices)
        return pltpu.make_async_remote_copy(
            src_ref=answer_ref.at[g, pl.ds(pl.multiple_of(peer * share, share), share), :],
            dst_ref=out_ref.at[g, pl.ds(pl.multiple_of(here * share, share), share), :],
            send_sem=sems.at[0, g, offset],
            recv_sem=sems.at[1, g, offset],
            device_id={"score": peer},
            device_id_type=pl.DeviceIdType.MESH,
        )

    def stay(g):
        span = pl.ds(pl.multiple_of(here * share, share), share)
        return pltpu.make_async_copy(
            answer_ref.at[g, span, :], out_ref.at[g, span, :], local_sems.at[g]
        )

    for head in range(HEAD_GROUP):
        change_ref[pl.ds(head, slots, stride=HEAD_GROUP), :] = lax.dot_general(
            masked_ref[...],
            up_ref[head * HEAD_SIZE : (head + 1) * HEAD_SIZE, :],
            (((1,), (1,)), ((), ())),
            preferred_element_type=jnp.float32,
        )
    keys = key_ref[...].reshape(TOKEN_SPAN, HEAD_SIZE)
    values = value_ref[...].reshape(TOKEN_SPAN, HEAD_SIZE)
    bias = bias_ref[...]

    def spread(rows):
        wide = rows.astype(jnp.float32)[:, None, :]
        return jnp.broadcast_to(wide, (rows.shape[0], HEAD_GROUP, HEAD_SIZE)).reshape(
            rows.shape[0] * HEAD_GROUP, HEAD_SIZE
        )

    for start in range(0, slots * HEAD_GROUP, CHUNK):
        part = slice(start, start + CHUNK)
        part_slots = slice(start // HEAD_GROUP, (start + CHUNK) // HEAD_GROUP)
        query = (frozen_ref[part, :].astype(jnp.float32) + 2.0 * change_ref[part, :]).astype(
            jnp.bfloat16
        )
        scores = (
            lax.dot_general(
                query, keys, (((1,), (1,)), ((), ())), preferred_element_type=jnp.float32
            )
            * SCORE_SCALE
            + bias
        )
        own = (
            jnp.sum(
                query.astype(jnp.float32) * spread(self_key_ref[part_slots, :]), 1, keepdims=True
            )
            * SCORE_SCALE
        )
        top = jnp.maximum(jnp.max(scores, 1, keepdims=True), own)
        weights = jnp.exp2(scores - top)
        self_weight = jnp.exp2(own - top)
        inverse = 1.0 / (jnp.sum(weights, 1, keepdims=True) + self_weight)
        mixed = jnp.dot(
            (weights * inverse).astype(jnp.bfloat16), values, preferred_element_type=jnp.float32
        )
        self_weight = (self_weight * inverse).astype(jnp.bfloat16).astype(jnp.float32)
        answer_ref[turn, part, :] = (mixed + self_weight * spread(self_value_ref[part_slots, :])).astype(
            jnp.bfloat16
        )

    @pl.when(turn == 0)
    def _():
        pl.semaphore_wait(barrier, devices - 1)

    stay(turn).start()

    @pl.loop(0, devices - 1)
    def _(peer):
        back(turn, lax.rem(peer + devices // 2 - 1, devices - 1) + 1).start()

    @pl.when(turn == KEY_VALUE_HEADS - 1)
    def _():
        for g in range(KEY_VALUE_HEADS):
            stay(g).wait()

            @pl.loop(1, devices)
            def _(offset):
                back(g, offset).wait()


def attend(devices, frozen, masked, up, keys, values, self_rows, bias):
    slots, columns = masked.shape
    items = slots * HEAD_GROUP
    head_blocks = (MAXB, BLOCK_TOKENS, HEAD_SIZE)
    return pl.pallas_call(
        functools.partial(attend_kernel, devices),
        grid=(KEY_VALUE_HEADS,),
        in_specs=[
            pl.BlockSpec((items, HEAD_SIZE), lambda g: (0, g)),
            pl.BlockSpec((slots, columns), lambda g: (0, 0)),
            pl.BlockSpec((HEAD_GROUP * HEAD_SIZE, columns), lambda g: (g, 0)),
            pl.BlockSpec(head_blocks, lambda g: (0, 0, g)),
            pl.BlockSpec(head_blocks, lambda g: (0, 0, g)),
            pl.BlockSpec((slots, HEAD_SIZE), lambda g: (0, g)),
            pl.BlockSpec((slots, HEAD_SIZE), lambda g: (0, KEY_VALUE_HEADS + g)),
            pl.BlockSpec((1, TOKEN_SPAN), lambda g: (0, 0)),
        ],
        out_specs=pl.BlockSpec(memory_space=pl.ANY),
        out_shape=jax.ShapeDtypeStruct((KEY_VALUE_HEADS, items, HEAD_SIZE), jnp.bfloat16),
        scratch_shapes=[
            pltpu.VMEM((items, HEAD_SIZE), jnp.float32),
            pltpu.VMEM((KEY_VALUE_HEADS, items, HEAD_SIZE), jnp.bfloat16),
            pltpu.SemaphoreType.DMA((2, KEY_VALUE_HEADS, devices)),
            pltpu.SemaphoreType.DMA((KEY_VALUE_HEADS,)),
        ],
        compiler_params=pltpu.CompilerParams(
            collective_id=1, has_side_effects=True, vmem_limit_bytes=48 * 1024 * 1024
        ),
        name="attend",
    )(frozen, masked, up, keys, values, self_rows, self_rows, bias)


def ring_chip(place, chips):
    half = chips // 2
    side = lax.div(place, half)
    step = lax.rem(place, half)
    return 2 * (step * (1 - side) + (half - 1 - step) * side) + side


def feed_kernel(
    devices, hidden_ref, chosen_ref, chooser_ref, down_ref, up_ref, frozen_ref, self_ref,
    up_full, frozen_out, self_out, masked_out,
    down_full, total, masked_send, pieces, row_sems, local_sems,
):
    chips = devices // 2
    group = lax.axis_index("groups")
    here = lax.axis_index("score")
    chip, core = lax.div(here, 2), lax.rem(here, 2)
    step_of, side = lax.div(chip, 2), lax.rem(chip, 2)
    place = side * (chips - 1 - step_of) + (1 - side) * step_of
    after = ring_chip(lax.rem(place + 1, chips), chips) * 2 + core
    before = ring_chip(lax.rem(place + chips - 1, chips), chips) * 2 + core
    sibling = chip * 2 + 1 - core
    next_on = (after, before)
    sources = (down_ref, up_ref)
    fulls = (down_full, up_full)
    parts = HEAD_SIZE

    barrier = pltpu.get_barrier_semaphore()

    @pl.loop(1, devices)
    def _(offset):
        pl.semaphore_signal(
            barrier, inc=1, device_id={"score": lax.rem(here + offset, devices)},
            device_id_type=pl.DeviceIdType.MESH,
        )

    pl.semaphore_signal(
        barrier, inc=1, device_id={"groups": 1 - group}, device_id_type=pl.DeviceIdType.MESH
    )
    pl.semaphore_wait(barrier, devices)

    def remote(source, target, send, recv, device):
        return pltpu.make_async_remote_copy(
            src_ref=source, dst_ref=target, send_sem=send, recv_sem=recv, device_id=device,
            device_id_type=pl.DeviceIdType.MESH,
        )

    def shard(a, owner, quarter=None):
        rows = sources[a].shape[0]
        span = pl.ds(pl.multiple_of(owner * rows, rows), rows)
        if quarter is None:
            return fulls[a].at[span, :]
        if rows % 64 == 0:
            size = rows // 4
            first = pl.multiple_of(owner * rows + quarter * size, size)
            return fulls[a].at[pl.ds(first, size), :]
        return fulls[a].at[span, pl.ds(pl.multiple_of(quarter * parts, parts), parts)]

    def origin(d, t):
        turn = place + chips - t if d == 0 else place + t
        return ring_chip(lax.rem(turn, chips), chips)

    def ring(a, d, t):
        ref = shard(a, origin(d, t) * 2 + core, group * 2 + d)
        return remote(ref, ref, pieces.at[0, a, d, t], pieces.at[1, a, d, t], {"score": next_on[d]})

    def beside(a, d, t):
        ref = shard(a, origin(d, t) * 2 + core, group * 2 + d)
        return remote(ref, ref, pieces.at[2, a, d, t], pieces.at[3, a, d, t], {"score": sibling})

    def across(a, d, t):
        ref = shard(a, origin(d, t) * 2 + core, group * 2 + d)
        return remote(ref, ref, pieces.at[4, a, d, t], pieces.at[5, a, d, t], {"groups": 1 - group})

    def onward(a, d, t):
        ref = shard(a, origin(d, t) * 2 + core, (1 - group) * 2 + d)
        return remote(ref, ref, pieces.at[6, a, d, t], pieces.at[7, a, d, t], {"score": sibling})

    def whole(a):
        ref = shard(a, here)
        return remote(ref, ref, pieces.at[2, a, 0, 0], pieces.at[3, a, 0, 0], {"score": sibling})

    def rows_to(kind, offset):
        peer = lax.rem(here + offset, devices)
        source = (frozen_ref, self_ref, masked_send)[kind]
        target = (frozen_out, self_out, masked_out)[kind]
        size = source.shape[0] // devices
        return remote(
            source.at[pl.ds(pl.multiple_of(peer * size, size), size), :],
            target.at[pl.ds(pl.multiple_of(here * size, size), size), :],
            row_sems.at[0, kind, offset],
            row_sems.at[1, kind, offset],
            {"score": peer},
        )

    def rows_here(kind):
        source = (frozen_ref, self_ref, masked_send)[kind]
        target = (frozen_out, self_out, masked_out)[kind]
        size = source.shape[0] // devices
        span = pl.ds(pl.multiple_of(here * size, size), size)
        return pltpu.make_async_copy(source.at[span, :], target.at[span, :], local_sems.at[2 + kind])

    own = [pltpu.make_async_copy(sources[a], shard(a, here), local_sems.at[a]) for a in range(2)]
    for copy in own:
        copy.start()
    rows_here(0).start()
    rows_here(1).start()
    for copy in own:
        copy.wait()

    def begin(a):
        for d in range(2):
            ring(a, d, 0).start()
        whole(a).start()

    def step(a, t):
        for d in range(2):
            ring(a, d, t).wait_recv()

            @pl.when(t < chips - 2)
            def _():
                ring(a, d, t + 1).start()

            across(a, d, t + 1).start()
            beside(a, d, t + 1).start()

        @pl.when(t > 0)
        def _():
            for d in range(2):
                across(a, d, t).wait_recv()
                onward(a, d, t).start()

    def send_rows(turn):
        offset = lax.rem(turn + devices // 2 - 1, devices - 1) + 1
        rows_to(0, offset).start()
        rows_to(1, offset).start()

    def finish(a):
        for d in range(2):
            across(a, d, chips - 1).wait_recv()
            onward(a, d, chips - 1).start()
        whole(a).wait_recv()

        @pl.loop(1, chips)
        def _(t):
            for d in range(2):
                beside(a, d, t).wait_recv()
                onward(a, d, t).wait_recv()

    begin(0)
    begin(1)
    lag = min(LAG, chips - 1)

    @pl.loop(0, chips - 1)
    def _(t):
        step(0, t)

        @pl.when(t >= lag)
        def _():
            step(1, t - lag)

        for extra in range(PEERS):
            send_rows(PEERS * t + extra)

    @pl.loop(PEERS * (chips - 1), devices - 1)
    def _(turn):
        send_rows(turn)

    finish(0)

    total[...] = jnp.zeros_like(total)
    depth = hidden_ref.shape[1] // 8

    @pl.loop(0, 8)
    def _(k):
        span = pl.ds(pl.multiple_of(k * depth, depth), depth)
        total[...] += jnp.dot(
            hidden_ref[:, span], down_full[span, :], preferred_element_type=jnp.float32
        )

    masked = jnp.where(chosen_ref[...] != 0, total[...], 0.0).astype(jnp.bfloat16)
    masked_send[...] = jnp.dot(
        chooser_ref[...], masked, preferred_element_type=jnp.float32
    ).astype(jnp.bfloat16)
    rows_here(2).start()

    @pl.loop(1, devices)
    def _(offset):
        rows_to(2, offset).start()

    @pl.loop(chips - 1 - lag, chips - 1)
    def _(t):
        step(1, t)

    finish(1)

    for kind in range(3):
        rows_here(kind).wait()

    @pl.loop(1, devices)
    def _(offset):
        for kind in range(3):
            rows_to(kind, offset).wait()

    for a in range(2):
        whole(a).wait_send()
        for d in range(2):
            ring(a, d, 0).wait_send()

        @pl.loop(1, chips)
        def _(t):
            for d in range(2):
                @pl.when(t < chips - 1)
                def _():
                    ring(a, d, t).wait_send()

                beside(a, d, t).wait_send()
                across(a, d, t).wait_send()
                onward(a, d, t).wait_send()


def feed(devices, hidden, chosen, chooser, down, up, frozen, self_rows):
    rows, columns = chosen.shape
    padded = chooser.shape[0]
    vmem, anywhere = pl.BlockSpec(memory_space=pltpu.VMEM), pl.BlockSpec(memory_space=pl.ANY)
    shape = lambda *dims: jax.ShapeDtypeStruct(dims, jnp.bfloat16)
    return pl.pallas_call(
        functools.partial(feed_kernel, devices),
        in_specs=[vmem, vmem, vmem, anywhere, anywhere, anywhere, anywhere],
        out_specs=[anywhere] * 4,
        out_shape=[
            shape(up.shape[0] * devices, columns),
            shape(*frozen.shape),
            shape(*self_rows.shape),
            shape(padded, columns),
        ],
        scratch_shapes=[
            pltpu.VMEM((down.shape[0] * devices, columns), jnp.bfloat16),
            pltpu.VMEM((rows, columns), jnp.float32),
            pltpu.VMEM((padded, columns), jnp.bfloat16),
            pltpu.SemaphoreType.DMA((8, 2, 2, devices // 2)),
            pltpu.SemaphoreType.DMA((2, 3, devices)),
            pltpu.SemaphoreType.DMA((5,)),
        ],
        compiler_params=pltpu.CompilerParams(
            collective_id=0, has_side_effects=True, vmem_limit_bytes=40 * 1024 * 1024
        ),
        name="feed",
    )(hidden, chosen, chooser, down, up, frozen, self_rows)


def on_device(
    hidden,
    frozen_query_rows,
    answer_row_key,
    answer_row_value,
    row_request_index,
    row_checkpoint_index,
    request_device_owner,
    request_block_table,
    request_prefix_length,
    adapter_down_weight,
    adapter_up_weight,
    paged_key_blocks,
    paged_value_blocks,
):
    rows = hidden.shape[0]
    devices = lax.axis_size("score")
    capacity = max(2, (3 * rows + 2 * devices - 1) // (2 * devices))
    slots = devices * capacity
    width = frozen_query_rows.shape[1]
    kv_width = answer_row_key.shape[1]
    column_list = adapter_down_weight.shape[1]

    req_ids = jnp.arange(devices, dtype=jnp.int32)
    requests = row_request_index[:, 0]
    picked = requests[:, None] == req_ids[None, :]
    target = jnp.sum(jnp.where(picked, request_device_owner[None, :], 0), 1)
    hits = (target[:, None] == req_ids[None, :]).astype(jnp.int32)
    before = jnp.cumsum(hits, 0) - hits
    slot = target * capacity + jnp.sum(before * hits, 1)
    chooser = (jnp.arange(slots, dtype=jnp.int32)[:, None] == slot[None, :]).astype(jnp.bfloat16)

    def place(value_rows):
        return jnp.dot(chooser, value_rows, preferred_element_type=jnp.float32).astype(
            jnp.bfloat16
        )

    frozen = (
        place(frozen_query_rows)
        .reshape(slots, KEY_VALUE_HEADS, HEAD_GROUP, HEAD_SIZE)
        .transpose(0, 2, 1, 3)
        .reshape(slots * HEAD_GROUP, kv_width)
    )
    pitch = -(-capacity // 16) * 16
    wide_slot = slot // capacity * pitch + slot % capacity
    wide_ids = jnp.arange(devices * pitch, dtype=jnp.int32)
    wide = (wide_ids[:, None] == wide_slot[None, :]).astype(jnp.bfloat16)
    self_rows = place(jnp.concatenate([answer_row_key, answer_row_value], 1)).reshape(
        slots * 2 * KEY_VALUE_HEADS, HEAD_SIZE
    )
    column_owner = jnp.arange(column_list, dtype=jnp.int32) // ADAPTER_RANK
    chosen = (row_checkpoint_index[:, None] == column_owner[None, :]).astype(jnp.float32)
    here = lax.axis_index("score")
    local_req = jnp.sum(jnp.where(request_device_owner == here, req_ids, 0))
    order = lax.dynamic_index_in_dim(request_block_table, local_req, 0, keepdims=False)
    length = lax.dynamic_index_in_dim(request_prefix_length, local_req, 0, keepdims=False)
    blocks = jnp.arange(MAXB, dtype=jnp.int32)
    place_of = jnp.sum(jnp.where(order[None, :] == blocks[:, None], blocks[None, :], 0), 1)
    position = place_of[:, None] * BLOCK_TOKENS + jnp.arange(BLOCK_TOKENS, dtype=jnp.int32)[None, :]
    bias = jnp.where(position < length, 0.0, -jnp.inf).astype(jnp.float32).reshape(1, TOKEN_SPAN)

    frozen, bias = lax.optimization_barrier((frozen, bias))
    up, frozen, self_rows, masked = feed(
        devices, hidden, chosen, wide, adapter_down_weight, adapter_up_weight, frozen, self_rows
    )

    self_rows = self_rows.reshape(slots, 2 * kv_width)
    masked = masked.reshape(devices, pitch, column_list)[:, :capacity].reshape(slots, column_list)

    returned = attend(
        devices, frozen, masked, up, paged_key_blocks, paged_value_blocks, self_rows, bias
    )
    returned = returned.reshape(KEY_VALUE_HEADS, slots, HEAD_GROUP, HEAD_SIZE)[:, slot]
    return returned.transpose(1, 0, 2, 3).reshape(rows, width)


def solution(mesh):
    placed = (
        P(("groups", "score"), None),
        P(("groups", "score"), None),
        P(("groups", "score"), None),
        P(("groups", "score"), None),
        P(("groups", "score"), None),
        P(("groups", "score")),
        P("groups"),
        P("groups", None),
        P("groups"),
        P("score", None),
        P("score", None),
        P(("groups", "score"), None, None),
        P(("groups", "score"), None, None),
    )
    return jax.shard_map(
        on_device,
        mesh=mesh,
        in_specs=placed,
        out_specs=P(("groups", "score"), None),
        check_vma=False,
    )
```

```python
import functools

import jax
import jax.numpy as jnp
from jax import lax
from jax.experimental import pallas as pl
from jax.experimental.pallas import tpu as pltpu
from jax.sharding import PartitionSpec as P

QUERY_HEADS = 32
KEY_VALUE_HEADS = 4
HEAD_GROUP = QUERY_HEADS // KEY_VALUE_HEADS
HEAD_SIZE = 128
ADAPTER_RANK = 64
BLOCK_TOKENS = 128
MAXB = 12
TOKEN_SPAN = MAXB * BLOCK_TOKENS
SCORE_SCALE = 1.4426950408889634 / HEAD_SIZE**0.5
CHUNK = 256
LAG = 2
PEERS = 1


def attend_kernel(
    devices, frozen_ref, masked_ref, up_ref, key_ref, value_ref, self_key_ref, self_value_ref,
    owner_ref, table_ref, length_ref,
    out_ref, change_ref, answer_ref, sems, local_sems,
):
    slots = masked_ref.shape[0]
    share = slots * HEAD_GROUP // devices
    here = lax.axis_index("score")
    turn = pl.program_id(0)
    barrier = pltpu.get_barrier_semaphore()

    @pl.when(turn == 0)
    def _():
        @pl.loop(1, devices)
        def _(offset):
            pl.semaphore_signal(
                barrier, inc=1, device_id={"score": lax.rem(here + offset, devices)},
                device_id_type=pl.DeviceIdType.MESH,
            )

    def back(g, offset):
        peer = lax.rem(here + offset, devices)
        return pltpu.make_async_remote_copy(
            src_ref=answer_ref.at[g, pl.ds(pl.multiple_of(peer * share, share), share), :],
            dst_ref=out_ref.at[g, pl.ds(pl.multiple_of(here * share, share), share), :],
            send_sem=sems.at[0, g, offset],
            recv_sem=sems.at[1, g, offset],
            device_id={"score": peer},
            device_id_type=pl.DeviceIdType.MESH,
        )

    def stay(g):
        span = pl.ds(pl.multiple_of(here * share, share), share)
        return pltpu.make_async_copy(
            answer_ref.at[g, span, :], out_ref.at[g, span, :], local_sems.at[g]
        )

    for head in range(HEAD_GROUP):
        change_ref[pl.ds(head, slots, stride=HEAD_GROUP), :] = lax.dot_general(
            masked_ref[...],
            up_ref[head * HEAD_SIZE : (head + 1) * HEAD_SIZE, :],
            (((1,), (1,)), ((), ())),
            preferred_element_type=jnp.float32,
        )
    keys = key_ref[...].reshape(TOKEN_SPAN, HEAD_SIZE)
    values = value_ref[...].reshape(TOKEN_SPAN, HEAD_SIZE)
    mine = owner_ref[...] == here
    token = lax.broadcasted_iota(jnp.int32, (1, TOKEN_SPAN), 1)
    block = lax.div(token, BLOCK_TOKENS)
    position = lax.rem(token, BLOCK_TOKENS)
    for j in range(MAXB):
        stored = jnp.sum(jnp.where(mine, table_ref[:, j : j + 1], 0), 0, keepdims=True)
        position += jnp.where(block == stored, j * BLOCK_TOKENS, 0)
    length = jnp.sum(jnp.where(mine, length_ref[...], 0), 0, keepdims=True)
    bias = jnp.where(position < length, 0.0, -jnp.inf)

    def spread(rows):
        wide = rows.astype(jnp.float32)[:, None, :]
        return jnp.broadcast_to(wide, (rows.shape[0], HEAD_GROUP, HEAD_SIZE)).reshape(
            rows.shape[0] * HEAD_GROUP, HEAD_SIZE
        )

    for start in range(0, slots * HEAD_GROUP, CHUNK):
        part = slice(start, start + CHUNK)
        part_slots = slice(start // HEAD_GROUP, (start + CHUNK) // HEAD_GROUP)
        query = (frozen_ref[part, :].astype(jnp.float32) + 2.0 * change_ref[part, :]).astype(
            jnp.bfloat16
        )
        scores = (
            lax.dot_general(
                query, keys, (((1,), (1,)), ((), ())), preferred_element_type=jnp.float32
            )
            * SCORE_SCALE
            + bias
        )
        own = (
            jnp.sum(
                query.astype(jnp.float32) * spread(self_key_ref[part_slots, :]), 1, keepdims=True
            )
            * SCORE_SCALE
        )
        top = jnp.maximum(jnp.max(scores, 1, keepdims=True), own)
        weights = jnp.exp2(scores - top)
        self_weight = jnp.exp2(own - top)
        inverse = 1.0 / (jnp.sum(weights, 1, keepdims=True) + self_weight)
        mixed = jnp.dot(
            (weights * inverse).astype(jnp.bfloat16), values, preferred_element_type=jnp.float32
        )
        self_weight = (self_weight * inverse).astype(jnp.bfloat16).astype(jnp.float32)
        answer_ref[turn, part, :] = (mixed + self_weight * spread(self_value_ref[part_slots, :])).astype(
            jnp.bfloat16
        )

    @pl.when(turn == 0)
    def _():
        pl.semaphore_wait(barrier, devices - 1)

    stay(turn).start()

    @pl.loop(0, devices - 1)
    def _(peer):
        back(turn, lax.rem(peer + devices // 2 - 1, devices - 1) + 1).start()

    @pl.when(turn == KEY_VALUE_HEADS - 1)
    def _():
        for g in range(KEY_VALUE_HEADS):
            stay(g).wait()

            @pl.loop(1, devices)
            def _(offset):
                back(g, offset).wait()


def attend(devices, frozen, masked, up, keys, values, self_rows, owner, table, length):
    slots, columns = masked.shape
    items = slots * HEAD_GROUP
    head_blocks = (MAXB, BLOCK_TOKENS, HEAD_SIZE)
    return pl.pallas_call(
        functools.partial(attend_kernel, devices),
        grid=(KEY_VALUE_HEADS,),
        in_specs=[
            pl.BlockSpec((items, HEAD_SIZE), lambda g: (0, g)),
            pl.BlockSpec((slots, columns), lambda g: (0, 0)),
            pl.BlockSpec((HEAD_GROUP * HEAD_SIZE, columns), lambda g: (g, 0)),
            pl.BlockSpec(head_blocks, lambda g: (0, 0, g)),
            pl.BlockSpec(head_blocks, lambda g: (0, 0, g)),
            pl.BlockSpec((slots, HEAD_SIZE), lambda g: (0, g)),
            pl.BlockSpec((slots, HEAD_SIZE), lambda g: (0, KEY_VALUE_HEADS + g)),
            pl.BlockSpec(owner.shape, lambda g: (0, 0)),
            pl.BlockSpec(table.shape, lambda g: (0, 0)),
            pl.BlockSpec(length.shape, lambda g: (0, 0)),
        ],
        out_specs=pl.BlockSpec(memory_space=pl.ANY),
        out_shape=jax.ShapeDtypeStruct((KEY_VALUE_HEADS, items, HEAD_SIZE), jnp.bfloat16),
        scratch_shapes=[
            pltpu.VMEM((items, HEAD_SIZE), jnp.float32),
            pltpu.VMEM((KEY_VALUE_HEADS, items, HEAD_SIZE), jnp.bfloat16),
            pltpu.SemaphoreType.DMA((2, KEY_VALUE_HEADS, devices)),
            pltpu.SemaphoreType.DMA((KEY_VALUE_HEADS,)),
        ],
        compiler_params=pltpu.CompilerParams(
            collective_id=1, has_side_effects=True, vmem_limit_bytes=48 * 1024 * 1024
        ),
        name="attend",
    )(frozen, masked, up, keys, values, self_rows, self_rows, owner, table, length)


def ring_chip(place, chips):
    half = chips // 2
    side = lax.div(place, half)
    step = lax.rem(place, half)
    return 2 * (step * (1 - side) + (half - 1 - step) * side) + side


def feed_kernel(
    devices, hidden_ref, chosen_ref, chooser_ref, down_ref, up_ref, frozen_ref, self_ref,
    up_full, frozen_out, self_out, masked_out,
    down_full, total, masked_send, pieces, row_sems, local_sems,
):
    chips = devices // 2
    group = lax.axis_index("groups")
    here = lax.axis_index("score")
    chip, core = lax.div(here, 2), lax.rem(here, 2)
    step_of, side = lax.div(chip, 2), lax.rem(chip, 2)
    place = side * (chips - 1 - step_of) + (1 - side) * step_of
    after = ring_chip(lax.rem(place + 1, chips), chips) * 2 + core
    before = ring_chip(lax.rem(place + chips - 1, chips), chips) * 2 + core
    sibling = chip * 2 + 1 - core
    next_on = (after, before)
    sources = (down_ref, up_ref)
    fulls = (down_full, up_full)
    parts = HEAD_SIZE

    barrier = pltpu.get_barrier_semaphore()

    @pl.loop(1, devices)
    def _(offset):
        pl.semaphore_signal(
            barrier, inc=1, device_id={"score": lax.rem(here + offset, devices)},
            device_id_type=pl.DeviceIdType.MESH,
        )

    pl.semaphore_signal(
        barrier, inc=1, device_id={"groups": 1 - group}, device_id_type=pl.DeviceIdType.MESH
    )
    pl.semaphore_wait(barrier, devices)

    def remote(source, target, send, recv, device):
        return pltpu.make_async_remote_copy(
            src_ref=source, dst_ref=target, send_sem=send, recv_sem=recv, device_id=device,
            device_id_type=pl.DeviceIdType.MESH,
        )

    def shard(a, owner, quarter=None):
        rows = sources[a].shape[0]
        span = pl.ds(pl.multiple_of(owner * rows, rows), rows)
        if quarter is None:
            return fulls[a].at[span, :]
        if rows % 64 == 0:
            size = rows // 4
            first = pl.multiple_of(owner * rows + quarter * size, size)
            return fulls[a].at[pl.ds(first, size), :]
        return fulls[a].at[span, pl.ds(pl.multiple_of(quarter * parts, parts), parts)]

    def origin(d, t):
        turn = place + chips - t if d == 0 else place + t
        return ring_chip(lax.rem(turn, chips), chips)

    def ring(a, d, t):
        ref = shard(a, origin(d, t) * 2 + core, group * 2 + d)
        return remote(ref, ref, pieces.at[0, a, d, t], pieces.at[1, a, d, t], {"score": next_on[d]})

    def beside(a, d, t):
        ref = shard(a, origin(d, t) * 2 + core, group * 2 + d)
        return remote(ref, ref, pieces.at[2, a, d, t], pieces.at[3, a, d, t], {"score": sibling})

    def across(a, d, t):
        ref = shard(a, origin(d, t) * 2 + core, group * 2 + d)
        return remote(ref, ref, pieces.at[4, a, d, t], pieces.at[5, a, d, t], {"groups": 1 - group})

    def onward(a, d, t):
        ref = shard(a, origin(d, t) * 2 + core, (1 - group) * 2 + d)
        return remote(ref, ref, pieces.at[6, a, d, t], pieces.at[7, a, d, t], {"score": sibling})

    def whole(a):
        ref = shard(a, here)
        return remote(ref, ref, pieces.at[2, a, 0, 0], pieces.at[3, a, 0, 0], {"score": sibling})

    def rows_to(kind, offset):
        peer = lax.rem(here + offset, devices)
        source = (frozen_ref, self_ref, masked_send)[kind]
        target = (frozen_out, self_out, masked_out)[kind]
        size = source.shape[0] // devices
        return remote(
            source.at[pl.ds(pl.multiple_of(peer * size, size), size), :],
            target.at[pl.ds(pl.multiple_of(here * size, size), size), :],
            row_sems.at[0, kind, offset],
            row_sems.at[1, kind, offset],
            {"score": peer},
        )

    def rows_here(kind):
        source = (frozen_ref, self_ref, masked_send)[kind]
        target = (frozen_out, self_out, masked_out)[kind]
        size = source.shape[0] // devices
        span = pl.ds(pl.multiple_of(here * size, size), size)
        return pltpu.make_async_copy(source.at[span, :], target.at[span, :], local_sems.at[2 + kind])

    own = [pltpu.make_async_copy(sources[a], shard(a, here), local_sems.at[a]) for a in range(2)]
    for copy in own:
        copy.start()
    rows_here(0).start()
    rows_here(1).start()
    for copy in own:
        copy.wait()

    def begin(a):
        for d in range(2):
            ring(a, d, 0).start()
        whole(a).start()

    def step(a, t):
        for d in range(2):
            ring(a, d, t).wait_recv()

            @pl.when(t < chips - 2)
            def _():
                ring(a, d, t + 1).start()

            across(a, d, t + 1).start()
            beside(a, d, t + 1).start()

        @pl.when(t > 0)
        def _():
            for d in range(2):
                across(a, d, t).wait_recv()
                onward(a, d, t).start()

    def send_rows(turn):
        offset = lax.rem(turn + devices // 2 - 1, devices - 1) + 1
        rows_to(0, offset).start()
        rows_to(1, offset).start()

    def finish(a):
        for d in range(2):
            across(a, d, chips - 1).wait_recv()
            onward(a, d, chips - 1).start()
        whole(a).wait_recv()

        @pl.loop(1, chips)
        def _(t):
            for d in range(2):
                beside(a, d, t).wait_recv()
                onward(a, d, t).wait_recv()

    begin(0)
    begin(1)
    lag = min(LAG, chips - 1)

    @pl.loop(0, chips - 1)
    def _(t):
        step(0, t)

        @pl.when(t >= lag)
        def _():
            step(1, t - lag)

        for extra in range(PEERS):
            send_rows(PEERS * t + extra)

    @pl.loop(PEERS * (chips - 1), devices - 1)
    def _(turn):
        send_rows(turn)

    finish(0)

    total[...] = jnp.zeros_like(total)
    depth = hidden_ref.shape[1] // 8

    @pl.loop(0, 8)
    def _(k):
        span = pl.ds(pl.multiple_of(k * depth, depth), depth)
        total[...] += jnp.dot(
            hidden_ref[:, span], down_full[span, :], preferred_element_type=jnp.float32
        )

    masked = jnp.where(chosen_ref[...] != 0, total[...], 0.0).astype(jnp.bfloat16)
    masked_send[...] = jnp.dot(
        chooser_ref[...], masked, preferred_element_type=jnp.float32
    ).astype(jnp.bfloat16)
    rows_here(2).start()

    @pl.loop(1, devices)
    def _(offset):
        rows_to(2, offset).start()

    @pl.loop(chips - 1 - lag, chips - 1)
    def _(t):
        step(1, t)

    finish(1)

    for kind in range(3):
        rows_here(kind).wait()

    @pl.loop(1, devices)
    def _(offset):
        for kind in range(3):
            rows_to(kind, offset).wait()

    for a in range(2):
        whole(a).wait_send()
        for d in range(2):
            ring(a, d, 0).wait_send()

        @pl.loop(1, chips)
        def _(t):
            for d in range(2):
                @pl.when(t < chips - 1)
                def _():
                    ring(a, d, t).wait_send()

                beside(a, d, t).wait_send()
                across(a, d, t).wait_send()
                onward(a, d, t).wait_send()


def feed(devices, hidden, chosen, chooser, down, up, frozen, self_rows):
    rows, columns = chosen.shape
    padded = chooser.shape[0]
    vmem, anywhere = pl.BlockSpec(memory_space=pltpu.VMEM), pl.BlockSpec(memory_space=pl.ANY)
    shape = lambda *dims: jax.ShapeDtypeStruct(dims, jnp.bfloat16)
    return pl.pallas_call(
        functools.partial(feed_kernel, devices),
        in_specs=[vmem, vmem, vmem, anywhere, anywhere, anywhere, anywhere],
        out_specs=[anywhere] * 4,
        out_shape=[
            shape(up.shape[0] * devices, columns),
            shape(*frozen.shape),
            shape(*self_rows.shape),
            shape(padded, columns),
        ],
        scratch_shapes=[
            pltpu.VMEM((down.shape[0] * devices, columns), jnp.bfloat16),
            pltpu.VMEM((rows, columns), jnp.float32),
            pltpu.VMEM((padded, columns), jnp.bfloat16),
            pltpu.SemaphoreType.DMA((8, 2, 2, devices // 2)),
            pltpu.SemaphoreType.DMA((2, 3, devices)),
            pltpu.SemaphoreType.DMA((5,)),
        ],
        compiler_params=pltpu.CompilerParams(
            collective_id=0, has_side_effects=True, vmem_limit_bytes=40 * 1024 * 1024
        ),
        name="feed",
    )(hidden, chosen, chooser, down, up, frozen, self_rows)


def on_device(
    hidden,
    frozen_query_rows,
    answer_row_key,
    answer_row_value,
    row_request_index,
    row_checkpoint_index,
    request_device_owner,
    request_block_table,
    request_prefix_length,
    adapter_down_weight,
    adapter_up_weight,
    paged_key_blocks,
    paged_value_blocks,
):
    rows = hidden.shape[0]
    devices = lax.axis_size("score")
    capacity = max(2, (3 * rows + 2 * devices - 1) // (2 * devices))
    slots = devices * capacity
    width = frozen_query_rows.shape[1]
    kv_width = answer_row_key.shape[1]
    column_list = adapter_down_weight.shape[1]

    req_ids = jnp.arange(devices, dtype=jnp.int32)
    requests = row_request_index[:, 0]
    picked = requests[:, None] == req_ids[None, :]
    target = jnp.sum(jnp.where(picked, request_device_owner[None, :], 0), 1)
    hits = (target[:, None] == req_ids[None, :]).astype(jnp.int32)
    before = jnp.cumsum(hits, 0) - hits
    slot = target * capacity + jnp.sum(before * hits, 1)
    chooser = (jnp.arange(slots, dtype=jnp.int32)[:, None] == slot[None, :]).astype(jnp.bfloat16)

    def place(value_rows):
        return jnp.dot(chooser, value_rows, preferred_element_type=jnp.float32).astype(
            jnp.bfloat16
        )

    frozen = (
        place(frozen_query_rows)
        .reshape(slots, KEY_VALUE_HEADS, HEAD_GROUP, HEAD_SIZE)
        .transpose(0, 2, 1, 3)
        .reshape(slots * HEAD_GROUP, kv_width)
    )
    pitch = -(-capacity // 16) * 16
    wide_slot = slot // capacity * pitch + slot % capacity
    wide_ids = jnp.arange(devices * pitch, dtype=jnp.int32)
    wide = (wide_ids[:, None] == wide_slot[None, :]).astype(jnp.bfloat16)
    self_rows = place(jnp.concatenate([answer_row_key, answer_row_value], 1)).reshape(
        slots * 2 * KEY_VALUE_HEADS, HEAD_SIZE
    )
    column_owner = jnp.arange(column_list, dtype=jnp.int32) // ADAPTER_RANK
    chosen = (row_checkpoint_index[:, None] == column_owner[None, :]).astype(jnp.float32)
    up, frozen, self_rows, masked = feed(
        devices, hidden, chosen, wide, adapter_down_weight, adapter_up_weight, frozen, self_rows
    )

    self_rows = self_rows.reshape(slots, 2 * kv_width)
    masked = masked.reshape(devices, pitch, column_list)[:, :capacity].reshape(slots, column_list)

    returned = attend(
        devices,
        frozen,
        masked,
        up,
        paged_key_blocks,
        paged_value_blocks,
        self_rows,
        request_device_owner[:, None],
        request_block_table,
        request_prefix_length[:, None],
    )
    returned = returned.reshape(KEY_VALUE_HEADS, slots, HEAD_GROUP, HEAD_SIZE)[:, slot]
    return returned.transpose(1, 0, 2, 3).reshape(rows, width)


def solution(mesh):
    placed = (
        P(("groups", "score"), None),
        P(("groups", "score"), None),
        P(("groups", "score"), None),
        P(("groups", "score"), None),
        P(("groups", "score"), None),
        P(("groups", "score")),
        P("groups"),
        P("groups", None),
        P("groups"),
        P("score", None),
        P("score", None),
        P(("groups", "score"), None, None),
        P(("groups", "score"), None, None),
    )
    return jax.shard_map(
        on_device,
        mesh=mesh,
        in_specs=placed,
        out_specs=P(("groups", "score"), None),
        check_vma=False,
    )
```
